32 devices in a mesh: groups: 2 (over x), ep: 16 (over z, y, core).
Axes of the slice: x: 2, y: 2, z: 4, core: 2. Of those that a mesh axis runs over, the one named last changes fastest.
Arguments:
- hidden: bfloat16 [2, 128, 7168], P(None, ('groups', 'ep')), parts along dimension 1, may hold values from -6 to 6
- expert_ids: int32 [2, 128, 2], P(None, ('groups', 'ep')), parts along dimension 1, may hold values from 0 to 3, all different within a row; in each aligned block of 4 rows (0 to 3, 4 to 7, ..., all dimensions but the last counted through in order) at most 4 rows name the same one
- route_weight: float32 [2, 128, 2], P(None, ('groups', 'ep')), parts along dimension 1, may hold values from 0.1 to 1
- w_gate: bfloat16 [16, 7168, 256], P('ep'), may hold values from -0.0625 to 0.0625
- w_up: bfloat16 [16, 7168, 256], P('ep'), may hold values from -0.0625 to 0.0625
- w_down: bfloat16 [16, 256, 7168], P('ep'), may hold values from -0.1875 to 0.1875
Outputs:
- moe_output: bfloat16 [2, 128, 7168], P(None, ('groups', 'ep')), parts along dimension 1
The draws below stay inside these ranges and needn't reach their ends.
There are 2 independent parts, one for each index of `groups`. The reference program is written for one: setup_inputs(seed, part) draws one part's arguments, and reference() takes and returns one part's arrays. A program takes and returns all parts, laid end to end along the dimension named above; an argument that names none is the same for every part. Nothing has to cross between parts.
Inputs may be any that keep to these rules, and one draw needn't show every extreme that they name: `expert_ids`: each row names 2 different experts; in one step, the 4 rows of one device name no expert more than 4 times, and in some devices' rows an expert is named exactly 4 times.
All inputs are finite; a program needn't handle non-finite values.
Results may differ from the reference program's by a relative error of at most 0.0064.
Values may be sent and summed in bfloat16 or wider, within the bound.
No kernel may reach another device: no remote copies, remote signals or barrier semaphores. Data moves between devices by JAX's collectives and lax.ppermute only.
A program may use at most 128 MiB of HBM per device.

```python
import math
import jax
import jax.numpy as jnp
import numpy as np
from jax import lax

D = 7168
FF = 1024
FF_DEV = 256
STEPS = 2
TOK_DEV = 4
SPLIT = 4
EXPERTS = 4
TOP = 2
CAP = 4
TOKENS = 64
N_EP = 16


def level_of(own_key, dims, shards, smallest, largest):
    level = 1.0
    for position, blocks in shards:
        draws = jax.random.uniform(jax.random.fold_in(jax.random.fold_in(own_key, 6), position), (blocks,), jnp.float32, smallest / len(shards), largest / len(shards))
        level = level * jnp.repeat(jnp.exp(draws), dims[position] // blocks).reshape((-1,) + (1,) * (len(dims) - 1 - position))
    return level


def routed_block(rng, own, number, rows, amount, top, most, slope):
    ranking = jax.random.permutation(rng, amount)
    crowded, ordinary = shares(amount, rows * top, most, slope, True), shares(amount, rows * top, most, slope, False)
    places = jnp.arange(amount)

    def named(lengths, turn):
        used = int((lengths > 0).sum())
        fixed = max(1, used // 4)
        shifted = fixed + (places - fixed + turn * (used - fixed)) % max(1, amount - fixed)
        return jnp.zeros((amount,), jnp.int32).at[ranking[jnp.where(places < fixed, places, shifted)]].set(jnp.asarray(lengths, jnp.int32))

    lengths = jnp.where(number % 4 == 0, named(crowded, number // 4), named(ordinary, number - number // 4 - 1))
    mixed = jax.random.permutation(jax.random.fold_in(own, 3), amount)
    giver, sink = mixed[0:amount // 2 * 2:2], mixed[1:amount // 2 * 2:2]
    slack = jnp.minimum(lengths[giver] - 1, most - lengths[sink]) // 2
    slack = jnp.where((giver == ranking[0]) | (sink == ranking[0]) | (lengths[sink] == 0), 0, jnp.maximum(slack, 0))
    shifted = jax.random.randint(jax.random.fold_in(own, 4), (amount // 2,), 0, 1 << 20) % (slack + 1)
    lengths = lengths.at[giver].add(-shifted).at[sink].add(shifted)
    members = jnp.searchsorted(jnp.cumsum(lengths), jnp.arange(rows * top), side="right").astype(jnp.int32)
    listing = members.reshape(top, rows).T
    listing = listing[jax.random.permutation(jax.random.fold_in(own, 1), rows)]
    turn = jax.random.randint(jax.random.fold_in(own, 2), (rows, 1), 0, top)
    return jnp.take_along_axis(listing, (jnp.arange(top)[None, :] + turn) % top, axis=1)


def shares(count, total, most, skew, full):
    weights = [(1 << 20) // math.isqrt(rank ** skew) + 1 for rank in range(1, count + 1)]
    largest = most if full else min(most, max(-(-total // count), total * weights[0] // sum(weights)))
    least = 1 if total - largest >= count - 1 else 0
    given, spare = [largest] + [least] * (count - 1), total - largest - least * (count - 1)
    while spare > 0:
        candidates = [i for i in range(1, count) if given[i] < largest] or [i for i in range(1, count) if given[i] < most]
        pool, budget = sum([weights[i] for i in candidates]), spare
        for i in candidates:
            more = min(most - given[i], max(1, budget * weights[i] // pool), spare)
            given[i] = given[i] + more
            spare = spare - more
    return np.array(given)


def bell_draw(own_key, extent, deviation, most, split=(), kind=jnp.bfloat16):
    array = jax.random.normal(own_key, extent, jnp.float32) * deviation
    if len(split) > 0:
        array = level_of(own_key, extent, split, -0.22, 0.18) * array
    return jnp.clip(array, min=-most, max=most).astype(kind)


def setup_inputs(seed: int = 0, part: int = 0) -> dict:
    arg_keys = jax.random.split(jax.random.key(seed), 7)
    part_splits = jax.random.split(jax.random.fold_in(arg_keys[6], part), 7)
    hidden = bell_draw(part_splits[0], (STEPS, TOKENS, D), 1.0, 6.0, ((1, 16),))
    expert_ids_keys = jax.random.split(jax.random.fold_in(part_splits[1], 1), STEPS * TOKENS // TOK_DEV)
    expert_ids_turns = jax.random.permutation(jax.random.fold_in(part_splits[1], 3), STEPS * TOKENS // TOK_DEV)
    expert_ids = jax.vmap(lambda own, number: routed_block(jax.random.fold_in(part_splits[1], 2), own, number, TOK_DEV, EXPERTS, TOP, CAP, 2))(expert_ids_keys, expert_ids_turns).reshape((STEPS, TOKENS, TOP))
    route_weight = jnp.clip(jnp.exp(math.log(1.0) - 2.3025851 * jax.random.uniform(part_splits[2], (STEPS, TOKENS, TOP), jnp.float32) ** level_of(part_splits[2], (STEPS, TOKENS, TOP), ((1, 16),), -0.2, 0.2)), 0.1, 1.0)
    w_gate = bell_draw(arg_keys[3], (EXPERTS * SPLIT, D, FF_DEV), D ** -0.5, 0.0625, ((0, 16),))
    w_up = bell_draw(arg_keys[4], (EXPERTS * SPLIT, D, FF_DEV), D ** -0.5, 0.0625, ((0, 16),))
    w_down = bell_draw(arg_keys[5], (EXPERTS * SPLIT, FF_DEV, D), FF ** -0.5, 0.1875, ((0, 16),))
    return dict(hidden=hidden, expert_ids=expert_ids, route_weight=route_weight, w_gate=w_gate, w_up=w_up, w_down=w_down)


route_scale = 2.5


def expert_slice(rows, gate_w, up_w, down_w):
    gate_pre = jnp.dot(rows, gate_w, preferred_element_type=jnp.float32)
    up_pre = jnp.dot(rows, up_w, preferred_element_type=jnp.float32)
    slice_hidden = (jax.nn.silu(gate_pre) * up_pre).astype(jnp.bfloat16)
    return jnp.dot(slice_hidden, down_w, preferred_element_type=jnp.float32).astype(jnp.bfloat16)


def run_expert(operands):
    rows, gate_all, up_all, down_all = operands
    total = jnp.zeros((rows.shape[0], D), jnp.float32)
    for slice_index in range(SPLIT):
        total = total + expert_slice(rows, gate_all[slice_index], up_all[slice_index], down_all[slice_index]).astype(jnp.float32)
    return total.astype(jnp.bfloat16)


def reference(hidden, expert_ids, route_weight, w_gate, w_up, w_down):
    slots = N_EP * CAP
    gate_all = w_gate.reshape(EXPERTS, SPLIT, D, FF_DEV)
    up_all = w_up.reshape(EXPERTS, SPLIT, D, FF_DEV)
    down_all = w_down.reshape(EXPERTS, SPLIT, FF_DEV, D)
    outputs = []
    for step_index in range(STEPS):
        rows_now = hidden[step_index]
        flat_ids = expert_ids[step_index].reshape(-1).astype(jnp.int32)
        onehot = (flat_ids[:, None] == jnp.arange(EXPERTS, dtype=jnp.int32)[None, :]).astype(jnp.int32)
        slot_rank = jnp.sum((jnp.cumsum(onehot, axis=0) - 1) * onehot, axis=1).astype(jnp.int32)
        destination = (flat_ids * slots + slot_rank).astype(jnp.int32)
        owners = (jnp.arange(TOKENS * TOP, dtype=jnp.int32) // TOP).astype(jnp.int32)
        source_row = jnp.zeros((EXPERTS * slots,), jnp.int32).at[destination].set(owners)
        filled = jnp.zeros((EXPERTS * slots,), jnp.int32).at[destination].set(1)
        gathered = jnp.where(filled[:, None] == 1, jnp.take(rows_now, source_row, axis=0), jnp.zeros((), jnp.bfloat16))
        gathered = gathered.reshape(EXPERTS, slots, D)
        expert_rows = lax.map(run_expert, (gathered, gate_all, up_all, down_all)).reshape(EXPERTS * slots, D)
        picked = jnp.take(expert_rows, destination, axis=0).reshape(TOKENS, TOP, D).astype(jnp.float32)
        weights = route_weight[step_index]
        mix_weight = route_scale * weights / jnp.sum(weights, axis=-1, keepdims=True)
        outputs.append(jnp.sum(picked * mix_weight[..., None], axis=1).astype(jnp.bfloat16))
    return jnp.stack(outputs, 0)
```

```python
import jax
import jax.numpy as jnp
from jax import lax
from jax.sharding import PartitionSpec as P

FF = 1024


route_scale = 2.5


def swap(value, mask, devices):
    return lax.ppermute(value, "ep", [(i, i ^ mask) for i in range(devices)])


def local(hidden, expert_ids, route_weight, w_gate, w_up, w_down):
    step_count, token_count, features = hidden.shape
    slice_units = w_gate.shape[-1]
    splits = FF // slice_units
    devices = lax.axis_size("ep")
    experts = devices // splits
    row_count = step_count * token_count
    own_expert = lax.axis_index("ep") // splits

    own = hidden.reshape(row_count, features)
    blocks = [own] + [swap(own, splits * far, devices) for far in range(1, experts)]
    mask = splits // 2
    while mask:
        blocks = blocks + [swap(block, mask, devices) for block in blocks]
        mask //= 2
    rows = jnp.concatenate(blocks, axis=0)

    gate_pre = jnp.dot(rows, w_gate[0], preferred_element_type=jnp.float32)
    up_pre = jnp.dot(rows, w_up[0], preferred_element_type=jnp.float32)
    slice_hidden = (jax.nn.silu(gate_pre) * up_pre).astype(jnp.bfloat16)
    partial = jnp.dot(slice_hidden, w_down[0], preferred_element_type=jnp.float32)

    mask = 1
    while mask < splits:
        half = partial.shape[0] // 2
        other = swap(partial[half:].astype(jnp.bfloat16), mask, devices)
        partial = partial[:half] + other.astype(jnp.float32)
        mask *= 2
    expert_rows = partial.astype(jnp.bfloat16).reshape(experts, row_count, features)

    weights = route_scale * route_weight / jnp.sum(route_weight, axis=-1, keepdims=True)
    total = jnp.zeros((row_count, features), jnp.float32)
    for far in range(experts):
        back = expert_rows[far] if far == 0 else swap(expert_rows[far], splits * far, devices)
        share = jnp.sum(jnp.where(expert_ids == (own_expert ^ far), weights, 0.0), axis=-1)
        total = total + share.reshape(row_count, 1) * back.astype(jnp.float32)
    return total.astype(jnp.bfloat16).reshape(hidden.shape)


def solution(mesh):
    placed = (
        P(None, ("groups", "ep"), None),
        P(None, ("groups", "ep"), None),
        P(None, ("groups", "ep"), None),
        P("ep", None, None),
        P("ep", None, None),
        P("ep", None, None),
    )
    return jax.shard_map(
        local,
        mesh=mesh,
        in_specs=placed,
        out_specs=P(None, ("groups", "ep"), None),
        check_vma=False,
    )
```

```python
import functools

import jax
import jax.numpy as jnp
from jax import lax
from jax.experimental import pallas as pl
from jax.experimental.pallas import tpu as pltpu
from jax.sharding import PartitionSpec as P

FF = 1024


route_scale = 2.5
MIB = 1 << 20
VMEM = pl.BlockSpec(memory_space=pltpu.VMEM)


def swap(value, mask, devices):
    return lax.ppermute(value, "ep", [(i, i ^ mask) for i in range(devices)])


def largest_chunk(total, most):
    return max(c for c in range(128, most + 1, 128) if total % c == 0)


def expert_kernel(count, *refs):
    blocks, (gate_ref, up_ref, down_ref, send_ref, keep_ref, both) = refs[:count], refs[count:]
    features, units = gate_ref.shape[-2:]
    depth = largest_chunk(features, 1024)
    half = send_ref.shape[0]
    both[...] = jnp.zeros_like(both)

    @pl.loop(0, features // depth)
    def _(step):
        at = pl.ds(pl.multiple_of(step * depth, depth), depth)
        rows = jnp.concatenate([block[:, at] for block in blocks], axis=0)
        both[0] += jnp.dot(rows, gate_ref[at, :], preferred_element_type=jnp.float32)
        both[1] += jnp.dot(rows, up_ref[at, :], preferred_element_type=jnp.float32)

    gate_pre = both[0]
    slice_hidden = (gate_pre / (1 + jnp.exp(-gate_pre)) * both[1]).astype(jnp.bfloat16)

    @pl.loop(0, features // depth)
    def _(step):
        at = pl.ds(pl.multiple_of(step * depth, depth), depth)
        out = jnp.dot(slice_hidden, down_ref[:, at], preferred_element_type=jnp.float32)
        keep_ref[:, at] = out[:half]
        send_ref[:, at] = out[half:].astype(jnp.bfloat16)


def expert_slice(blocks, gate_w, up_w, down_w):
    features, units = gate_w.shape
    rows = sum(block.shape[0] for block in blocks)
    half = rows // 2
    return pl.pallas_call(
        functools.partial(expert_kernel, len(blocks)),
        out_shape=(
            jax.ShapeDtypeStruct((half, features), jnp.bfloat16),
            jax.ShapeDtypeStruct((half, features), jnp.float32),
        ),
        in_specs=[VMEM] * (len(blocks) + 3),
        out_specs=(VMEM, VMEM),
        scratch_shapes=[pltpu.VMEM((2, rows, units), jnp.float32)],
        compiler_params=pltpu.CompilerParams(vmem_limit_bytes=28 * MIB),
        cost_estimate=pl.CostEstimate(flops=6 * rows * units * features, bytes_accessed=6 * units * features, transcendentals=0),
        name="expert_slice",
    )(*blocks, gate_w, up_w, down_w)


def pass_kernel(rows_ref, *refs):
    refs[-1][...] = rows_ref[...]


def pass_rows(rows, *beside):
    return pl.pallas_call(
        pass_kernel,
        out_shape=jax.ShapeDtypeStruct(rows.shape, rows.dtype),
        in_specs=[VMEM] + [pl.BlockSpec(memory_space=pl.ANY)] * len(beside),
        out_specs=VMEM,
        compiler_params=pltpu.CompilerParams(vmem_limit_bytes=16 * MIB),
        name="pass_rows",
    )(rows, *[pltpu.with_memory_space_constraint(w, pltpu.HBM) for w in beside])


def add_kernel(size, places, keep_ref, *refs):
    terms, out_ref = refs[:-1], refs[-1]
    total = keep_ref[pl.ds(places[0] * size, size), :]
    for place, term in zip(places[1:], terms):
        total = total + term[pl.ds(place * size, size), :].astype(jnp.float32)
    out_ref[...] = total.astype(out_ref.dtype)


def add_rows(size, places, keep, *terms):
    features = keep.shape[1]
    return pl.pallas_call(
        functools.partial(add_kernel, size, places),
        out_shape=jax.ShapeDtypeStruct((size, features), jnp.bfloat16),
        in_specs=[VMEM] * (1 + len(terms)),
        out_specs=VMEM,
        compiler_params=pltpu.CompilerParams(vmem_limit_bytes=16 * MIB),
        cost_estimate=pl.CostEstimate(flops=size * features, bytes_accessed=8 * size * features, transcendentals=0),
        name="add_rows",
    )(keep, *terms)


def mix_kernel(share_ref, *refs):
    backs, out_ref = refs[:-1], refs[-1]
    steps, tokens, _ = out_ref.shape
    share = share_ref[...]
    total = share[:, 0:1] * backs[0][...].astype(jnp.float32)
    for far in range(1, len(backs)):
        total = total + share[:, far:far + 1] * backs[far][...].astype(jnp.float32)
    for step in range(steps):
        out_ref[step] = total[step * tokens:(step + 1) * tokens].astype(out_ref.dtype)


def mix(share, backs, shape):
    return pl.pallas_call(
        mix_kernel,
        out_shape=jax.ShapeDtypeStruct(shape, jnp.bfloat16),
        in_specs=[VMEM] * (1 + len(backs)),
        out_specs=VMEM,
        compiler_params=pltpu.CompilerParams(vmem_limit_bytes=16 * MIB),
        name="mix",
    )(share, *backs)


def local(hidden, expert_ids, route_weight, w_gate, w_up, w_down):
    step_count, token_count, features = hidden.shape
    slice_units = w_gate.shape[-1]
    splits = FF // slice_units
    devices = lax.axis_size("ep")
    experts = devices // splits
    row_count = step_count * token_count
    own_expert = lax.axis_index("ep") // splits

    own = hidden.reshape(row_count, features)
    blocks = {0: own}
    mask = devices // 2
    while mask:
        for key, block in list(blocks.items()):
            if key == devices // 2 and mask == devices // 4:
                block = pass_rows(block, w_gate, w_up, w_down)
            blocks[key + mask] = swap(block, mask, devices)
        mask //= 2
    order = [e * splits + y + c for c in (0, 1) for y in (0, 2) for e in range(experts)]
    send, keep = expert_slice([blocks[k] for k in order], w_gate[0], w_up[0], w_down[0])

    twin = swap(send, 1, devices)
    across = {}
    for far in reversed(range(experts)):
        across[far] = swap(add_rows(row_count, (experts + far, experts + far), keep, twin), 2, devices)
    backs = {}
    for far in reversed(range(experts)):
        rows = add_rows(row_count, (far, far, 0), keep, twin, across[far])
        backs[far] = swap(rows, splits * far, devices) if far else rows

    weights = route_scale * route_weight / jnp.sum(route_weight, axis=-1, keepdims=True)
    away = own_expert ^ jnp.arange(experts, dtype=jnp.int32)
    share = jnp.sum(jnp.where(expert_ids[..., None] == away, weights[..., None], 0.0), axis=-2)
    return mix(share.reshape(row_count, experts), [backs[far] for far in range(experts)], hidden.shape)


def solution(mesh):
    placed = (
        P(None, ("groups", "ep"), None),
        P(None, ("groups", "ep"), None),
        P(None, ("groups", "ep"), None),
        P("ep", None, None),
        P("ep", None, None),
        P("ep", None, None),
    )
    return jax.shard_map(
        local,
        mesh=mesh,
        in_specs=placed,
        out_specs=P(None, ("groups", "ep"), None),
        check_vma=False,
    )
```

```python
import functools

import jax
import jax.numpy as jnp
from jax import lax
from jax.experimental import pallas as pl
from jax.experimental.pallas import tpu as pltpu
from jax.sharding import PartitionSpec as P

FF = 1024


route_scale = 2.5
MIB = 1 << 20
VMEM = pl.BlockSpec(memory_space=pltpu.VMEM)


def swap(value, mask, devices):
    return lax.ppermute(value, "ep", [(i, i ^ mask) for i in range(devices)])


def largest_chunk(total, most):
    return max(c for c in range(128, most + 1, 128) if total % c == 0)


def in_steps(total, depth, unrolled):
    def run(body):
        if unrolled:
            for step in range(total // depth):
                body(pl.ds(step * depth, depth))
        else:
            pl.loop(0, total // depth)(lambda step: body(pl.ds(pl.multiple_of(step * depth, depth), depth)))

    return run


def expert_kernel(count, *refs):
    blocks, (gate_ref, up_ref, down_ref, send_ref, keep_ref, both) = refs[:count], refs[count:]
    features, units = gate_ref.shape[-2:]
    depth = largest_chunk(features, 1024)
    half = send_ref.shape[0]
    both[...] = jnp.zeros_like(both)

    @in_steps(features, depth, both.shape[1] <= 256)
    def _(at):
        rows = jnp.concatenate([block[:, at] for block in blocks], axis=0)
        both[0] += jnp.dot(rows, gate_ref[at, :], preferred_element_type=jnp.float32)
        both[1] += jnp.dot(rows, up_ref[at, :], preferred_element_type=jnp.float32)

    gate_pre = both[0]
    slice_hidden = (gate_pre / (1 + jnp.exp(-gate_pre)) * both[1]).astype(jnp.bfloat16)

    @in_steps(features, depth, both.shape[1] <= 256)
    def _(at):
        out = jnp.dot(slice_hidden, down_ref[:, at], preferred_element_type=jnp.float32)
        keep_ref[:, at] = out[:half]
        send_ref[:, at] = out[half:].astype(jnp.bfloat16)


def expert_slice(blocks, gate_w, up_w, down_w):
    features, units = gate_w.shape
    rows = sum(block.shape[0] for block in blocks)
    half = rows // 2
    return pl.pallas_call(
        functools.partial(expert_kernel, len(blocks)),
        out_shape=(
            jax.ShapeDtypeStruct((half, features), jnp.bfloat16),
            jax.ShapeDtypeStruct((half, features), jnp.float32),
        ),
        in_specs=[VMEM] * (len(blocks) + 3),
        out_specs=(VMEM, VMEM),
        scratch_shapes=[pltpu.VMEM((2, rows, units), jnp.float32)],
        compiler_params=pltpu.CompilerParams(vmem_limit_bytes=28 * MIB),
        cost_estimate=pl.CostEstimate(flops=6 * rows * units * features, bytes_accessed=6 * units * features, transcendentals=0),
        name="expert_slice",
    )(*blocks, gate_w, up_w, down_w)


def pass_kernel(rows_ref, *refs):
    refs[-1][...] = rows_ref[...]


def pass_rows(rows, *beside):
    return pl.pallas_call(
        pass_kernel,
        out_shape=jax.ShapeDtypeStruct(rows.shape, rows.dtype),
        in_specs=[VMEM] + [pl.BlockSpec(memory_space=pl.ANY)] * len(beside),
        out_specs=VMEM,
        compiler_params=pltpu.CompilerParams(vmem_limit_bytes=16 * MIB),
        name="pass_rows",
    )(rows, *[pltpu.with_memory_space_constraint(w, pltpu.HBM) for w in beside])


def add_kernel(size, places, keep_ref, *refs):
    terms, out_ref = refs[:-1], refs[-1]
    total = keep_ref[pl.ds(places[0] * size, size), :]
    for place, term in zip(places[1:], terms):
        total = total + term[pl.ds(place * size, size), :].astype(jnp.float32)
    out_ref[...] = total.astype(out_ref.dtype)


def add_rows(size, places, keep, *terms):
    features = keep.shape[1]
    return pl.pallas_call(
        functools.partial(add_kernel, size, places),
        out_shape=jax.ShapeDtypeStruct((size, features), jnp.bfloat16),
        in_specs=[VMEM] * (1 + len(terms)),
        out_specs=VMEM,
        compiler_params=pltpu.CompilerParams(vmem_limit_bytes=16 * MIB),
        cost_estimate=pl.CostEstimate(flops=size * features, bytes_accessed=8 * size * features, transcendentals=0),
        name="add_rows",
    )(keep, *terms)


def mix_kernel(share_ref, *refs):
    backs, out_ref = refs[:-1], refs[-1]
    steps, tokens, _ = out_ref.shape
    share = share_ref[...]
    total = share[:, 0:1] * backs[0][...].astype(jnp.float32)
    for far in range(1, len(backs)):
        total = total + share[:, far:far + 1] * backs[far][...].astype(jnp.float32)
    for step in range(steps):
        out_ref[step] = total[step * tokens:(step + 1) * tokens].astype(out_ref.dtype)


def mix(share, backs, shape):
    return pl.pallas_call(
        mix_kernel,
        out_shape=jax.ShapeDtypeStruct(shape, jnp.bfloat16),
        in_specs=[VMEM] * (1 + len(backs)),
        out_specs=VMEM,
        compiler_params=pltpu.CompilerParams(vmem_limit_bytes=16 * MIB),
        name="mix",
    )(share, *backs)


def local(hidden, expert_ids, route_weight, w_gate, w_up, w_down):
    step_count, token_count, features = hidden.shape
    slice_units = w_gate.shape[-1]
    splits = FF // slice_units
    devices = lax.axis_size("ep")
    experts = devices // splits
    row_count = step_count * token_count
    own_expert = lax.axis_index("ep") // splits

    own = hidden.reshape(row_count, features)
    blocks = {0: own}
    for key in sorted(range(1, devices), key=lambda key: (key.bit_count(), -key)):
        mask = splits if key == splits + 2 else key & -key
        block = blocks[key - mask]
        if key == devices // 2 + devices // 4:
            block, blocks[splits] = lax.optimization_barrier((block, blocks[splits]))
            block = pass_rows(block, w_gate, w_up, w_down)
        blocks[key] = swap(block, mask, devices)
    order = [e * splits + y + c for c in (0, 1) for y in (0, 2) for e in range(experts)]
    send, keep = expert_slice([blocks[k] for k in order], w_gate[0], w_up[0], w_down[0])

    twin = swap(send, 1, devices)
    across = {}
    for far in reversed(range(experts)):
        across[far] = swap(add_rows(row_count, (experts + far, experts + far), keep, twin), 2, devices)
    backs = {}
    for far in reversed(range(experts)):
        rows = add_rows(row_count, (far, far, 0), keep, twin, across[far])
        backs[far] = swap(rows, splits * far, devices) if far else rows

    weights = route_scale * route_weight / jnp.sum(route_weight, axis=-1, keepdims=True)
    away = own_expert ^ jnp.arange(experts, dtype=jnp.int32)
    share = jnp.sum(jnp.where(expert_ids[..., None] == away, weights[..., None], 0.0), axis=-2)
    return mix(share.reshape(row_count, experts), [backs[far] for far in range(experts)], hidden.shape)


def solution(mesh):
    placed = (
        P(None, ("groups", "ep"), None),
        P(None, ("groups", "ep"), None),
        P(None, ("groups", "ep"), None),
        P("ep", None, None),
        P("ep", None, None),
        P("ep", None, None),
    )
    return jax.shard_map(
        local,
        mesh=mesh,
        in_specs=placed,
        out_specs=P(None, ("groups", "ep"), None),
        check_vma=False,
    )
```

```python
import functools

import jax
import jax.numpy as jnp
from jax import lax
from jax.experimental import pallas as pl
from jax.experimental.pallas import tpu as pltpu
from jax.sharding import PartitionSpec as P

FF = 1024


route_scale = 2.5
MIB = 1 << 20
VMEM = pl.BlockSpec(memory_space=pltpu.VMEM)


def swap(value, mask, devices):
    return lax.ppermute(value, "ep", [(i, i ^ mask) for i in range(devices)])


def largest_chunk(total, most):
    return max(c for c in range(128, most + 1, 128) if total % c == 0)


def in_steps(total, depth, unrolled):
    def run(body):
        if unrolled:
            for step in range(total // depth):
                body(pl.ds(step * depth, depth))
        else:
            pl.loop(0, total // depth)(lambda step: body(pl.ds(pl.multiple_of(step * depth, depth), depth)))

    return run


def expert_kernel(count, *refs):
    blocks, (gate_ref, up_ref, down_ref, send_ref, keep_ref, both) = refs[:count], refs[count:]
    features, units = gate_ref.shape[-2:]
    depth = largest_chunk(features, 1024)
    half = send_ref.shape[0]
    both[...] = jnp.zeros_like(both)

    @in_steps(features, depth, both.shape[1] <= 256)
    def _(at):
        rows = jnp.concatenate([block[:, at] for block in blocks], axis=0)
        both[0] += jnp.dot(rows, gate_ref[at, :], preferred_element_type=jnp.float32)
        both[1] += jnp.dot(rows, up_ref[at, :], preferred_element_type=jnp.float32)

    gate_pre = both[0]
    slice_hidden = (gate_pre / (1 + jnp.exp(-gate_pre)) * both[1]).astype(jnp.bfloat16)

    @in_steps(features, depth, both.shape[1] <= 256)
    def _(at):
        out = jnp.dot(slice_hidden, down_ref[:, at], preferred_element_type=jnp.float32)
        keep_ref[:, at] = out[:half]
        send_ref[:, at] = out[half:].astype(jnp.bfloat16)


def expert_slice(blocks, gate_w, up_w, down_w):
    features, units = gate_w.shape
    rows = sum(block.shape[0] for block in blocks)
    half = rows // 2
    return pl.pallas_call(
        functools.partial(expert_kernel, len(blocks)),
        out_shape=(
            jax.ShapeDtypeStruct((half, features), jnp.bfloat16),
            jax.ShapeDtypeStruct((half, features), jnp.float32),
        ),
        in_specs=[VMEM] * (len(blocks) + 3),
        out_specs=(VMEM, VMEM),
        scratch_shapes=[pltpu.VMEM((2, rows, units), jnp.float32)],
        compiler_params=pltpu.CompilerParams(vmem_limit_bytes=28 * MIB),
        cost_estimate=pl.CostEstimate(flops=6 * rows * units * features, bytes_accessed=6 * units * features, transcendentals=0),
        name="expert_slice",
    )(*blocks, gate_w, up_w, down_w)


def pass_kernel(rows_ref, *refs):
    refs[-1][...] = rows_ref[...]


def pass_rows(rows, *beside):
    return pl.pallas_call(
        pass_kernel,
        out_shape=jax.ShapeDtypeStruct(rows.shape, rows.dtype),
        in_specs=[VMEM] + [pl.BlockSpec(memory_space=pl.ANY)] * len(beside),
        out_specs=VMEM,
        compiler_params=pltpu.CompilerParams(vmem_limit_bytes=16 * MIB),
        name="pass_rows",
    )(rows, *[pltpu.with_memory_space_constraint(w, pltpu.HBM) for w in beside])


def pack_kernel(*refs):
    refs[-1][...] = jnp.concatenate([ref[step] for ref in refs[:-1] for step in range(ref.shape[0])], axis=0)


def pack(blocks):
    steps, tokens, features = blocks[0].shape
    rows = len(blocks) * steps * tokens
    return pl.pallas_call(
        pack_kernel,
        out_shape=jax.ShapeDtypeStruct((rows, features), blocks[0].dtype),
        in_specs=[VMEM] * len(blocks),
        out_specs=VMEM,
        compiler_params=pltpu.CompilerParams(vmem_limit_bytes=16 * MIB),
        cost_estimate=pl.CostEstimate(flops=0, bytes_accessed=4 * rows * features, transcendentals=0),
        name="pack_rows",
    )(*blocks)


def add_kernel(size, places, keep_ref, *refs):
    terms, out_ref = refs[:-1], refs[-1]
    total = keep_ref[pl.ds(places[0] * size, size), :]
    for place, term in zip(places[1:], terms):
        total = total + term[pl.ds(place * size, size), :].astype(jnp.float32)
    out_ref[...] = total.astype(out_ref.dtype)


def add_rows(size, places, keep, *terms):
    features = keep.shape[1]
    return pl.pallas_call(
        functools.partial(add_kernel, size, places),
        out_shape=jax.ShapeDtypeStruct((size, features), jnp.bfloat16),
        in_specs=[VMEM] * (1 + len(terms)),
        out_specs=VMEM,
        compiler_params=pltpu.CompilerParams(vmem_limit_bytes=16 * MIB),
        cost_estimate=pl.CostEstimate(flops=size * features, bytes_accessed=8 * size * features, transcendentals=0),
        name="add_rows",
    )(keep, *terms)


def mix_kernel(fars, share_ref, *refs):
    backs, out_ref = refs[:-1], refs[-1]
    steps, tokens, _ = out_ref.shape
    share = share_ref[...]
    total = sum(share[:, far:far + 1] * back[...].astype(jnp.float32) for far, back in zip(fars, backs))
    for step in range(steps):
        out_ref[step] = total[step * tokens:(step + 1) * tokens].astype(out_ref.dtype)


def mix(share, backs, shape):
    return pl.pallas_call(
        functools.partial(mix_kernel, tuple(backs)),
        out_shape=jax.ShapeDtypeStruct(shape, jnp.bfloat16),
        in_specs=[VMEM] * (1 + len(backs)),
        out_specs=VMEM,
        compiler_params=pltpu.CompilerParams(vmem_limit_bytes=16 * MIB),
        name="mix",
    )(share, *backs.values())


def local(hidden, expert_ids, route_weight, w_gate, w_up, w_down):
    step_count, token_count, features = hidden.shape
    slice_units = w_gate.shape[-1]
    splits = FF // slice_units
    devices = lax.axis_size("ep")
    experts = devices // splits
    row_count = step_count * token_count
    own_expert = lax.axis_index("ep") // splits

    blocks = {0: hidden}
    for key in sorted(range(2, devices, 2), key=lambda key: (key.bit_count(), -key)):
        mask = splits if key == splits + 2 else key & -key
        block = blocks[key - mask]
        if key == devices // 2 + devices // 4:
            block, blocks[splits] = lax.optimization_barrier((block, blocks[splits]))
            block = pass_rows(block, w_gate, w_up, w_down)
        blocks[key] = swap(block, mask, devices)
    last = devices - splits
    batches = [
        ([*range(0, last, splits), 2], range(splits + 2, last, splits)),
        ([last, last + 2],),
    ]

    backs = {}
    for batch in [[keys for batch in batches for keys in batch]]:
        keep_rows = [pack([blocks[key] for key in keys]) for keys in batch]
        send_rows = [swap(rows, 1, devices) for rows in keep_rows]
        fars = [0, *range(3, experts), 1, 2]
        send, keep = expert_slice(keep_rows + send_rows, w_gate[0], w_up[0], w_down[0])
        twin = swap(send, 1, devices)
        keys = [key for group in batch for key in group]
        for far in reversed(fars):
            theirs, mine = keys.index(far * splits + 2), keys.index(far * splits)
            across = swap(add_rows(row_count, (theirs, theirs), keep, twin), 2, devices)
            rows = add_rows(row_count, (mine, mine, 0), keep, twin, across)
            backs[far] = swap(rows, splits * far, devices) if far else rows

    weights = route_scale * route_weight / jnp.sum(route_weight, axis=-1, keepdims=True)
    away = own_expert ^ jnp.arange(experts, dtype=jnp.int32)
    share = jnp.sum(jnp.where(expert_ids[..., None] == away, weights[..., None], 0.0), axis=-2)
    return mix(share.reshape(row_count, experts), {far: backs[far] for far in fars}, hidden.shape)


def solution(mesh):
    placed = (
        P(None, ("groups", "ep"), None),
        P(None, ("groups", "ep"), None),
        P(None, ("groups", "ep"), None),
        P("ep", None, None),
        P("ep", None, None),
        P("ep", None, None),
    )
    return jax.shard_map(
        local,
        mesh=mesh,
        in_specs=placed,
        out_specs=P(None, ("groups", "ep"), None),
        check_vma=False,
    )
```

```python
import functools

import jax
import jax.numpy as jnp
from jax import lax
from jax.experimental import pallas as pl
from jax.experimental.pallas import tpu as pltpu
from jax.sharding import PartitionSpec as P

FF = 1024


route_scale = 2.5
MIB = 1 << 20
VMEM = pl.BlockSpec(memory_space=pltpu.VMEM)


def swap(value, mask, devices):
    return lax.ppermute(value, "ep", [(i, i ^ mask) for i in range(devices)])


def largest_chunk(total, most):
    return max(c for c in range(128, most + 1, 128) if total % c == 0)


def in_steps(total, depth, unrolled):
    def run(body):
        if unrolled:
            for step in range(total // depth):
                body(pl.ds(step * depth, depth))
        else:
            pl.loop(0, total // depth)(lambda step: body(pl.ds(pl.multiple_of(step * depth, depth), depth)))

    return run


def expert_kernel(count, *refs):
    blocks, (gate_ref, up_ref, down_ref, send_ref, keep_ref, both) = refs[:count], refs[count:]
    features, units = gate_ref.shape[-2:]
    depth = largest_chunk(features, 1024)
    half = send_ref.shape[0]
    both[...] = jnp.zeros_like(both)

    @in_steps(features, depth, both.shape[1] <= 256)
    def _(at):
        rows = jnp.concatenate([block[:, at] for block in blocks], axis=0)
        both[0] += jnp.dot(rows, gate_ref[at, :], preferred_element_type=jnp.float32)
        both[1] += jnp.dot(rows, up_ref[at, :], preferred_element_type=jnp.float32)

    gate_pre = both[0]
    slice_hidden = (gate_pre / (1 + jnp.exp(-gate_pre)) * both[1]).astype(jnp.bfloat16)

    @in_steps(features, depth, both.shape[1] <= 256)
    def _(at):
        out = jnp.dot(slice_hidden, down_ref[:, at], preferred_element_type=jnp.float32)
        keep_ref[:, at] = out[:half]
        send_ref[:, at] = out[half:].astype(jnp.bfloat16)


def expert_slice(blocks, gate_w, up_w, down_w):
    features, units = gate_w.shape
    rows = sum(block.shape[0] for block in blocks)
    half = rows // 2
    return pl.pallas_call(
        functools.partial(expert_kernel, len(blocks)),
        out_shape=(
            jax.ShapeDtypeStruct((half, features), jnp.bfloat16),
            jax.ShapeDtypeStruct((half, features), jnp.float32),
        ),
        in_specs=[VMEM] * (len(blocks) + 3),
        out_specs=(VMEM, VMEM),
        scratch_shapes=[pltpu.VMEM((2, rows, units), jnp.float32)],
        compiler_params=pltpu.CompilerParams(vmem_limit_bytes=28 * MIB),
        cost_estimate=pl.CostEstimate(flops=6 * rows * units * features, bytes_accessed=6 * units * features, transcendentals=0),
        name="expert_slice",
    )(*blocks, gate_w, up_w, down_w)


def pass_kernel(rows_ref, *refs):
    refs[-1][...] = rows_ref[...]


def pass_rows(rows, *beside):
    return pl.pallas_call(
        pass_kernel,
        out_shape=jax.ShapeDtypeStruct(rows.shape, rows.dtype),
        in_specs=[VMEM] + [pl.BlockSpec(memory_space=pl.ANY)] * len(beside),
        out_specs=VMEM,
        compiler_params=pltpu.CompilerParams(vmem_limit_bytes=16 * MIB),
        name="pass_rows",
    )(rows, *[pltpu.with_memory_space_constraint(w, pltpu.HBM) for w in beside])


def pack_kernel(*refs):
    refs[-1][...] = jnp.concatenate([ref[step] for ref in refs[:-1] for step in range(ref.shape[0])], axis=0)


def pack(blocks):
    steps, tokens, features = blocks[0].shape
    rows = len(blocks) * steps * tokens
    return pl.pallas_call(
        pack_kernel,
        out_shape=jax.ShapeDtypeStruct((rows, features), blocks[0].dtype),
        in_specs=[VMEM] * len(blocks),
        out_specs=VMEM,
        compiler_params=pltpu.CompilerParams(vmem_limit_bytes=16 * MIB),
        cost_estimate=pl.CostEstimate(flops=0, bytes_accessed=4 * rows * features, transcendentals=0),
        name="pack_rows",
    )(*blocks)


def add_kernel(size, places, keep_ref, *refs):
    terms, out_ref = refs[:-1], refs[-1]
    total = keep_ref[pl.ds(places[0] * size, size), :]
    for place, term in zip(places[1:], terms):
        total = total + term[pl.ds(place * size, size), :].astype(jnp.float32)
    out_ref[...] = total.astype(out_ref.dtype)


def add_rows(size, places, keep, *terms):
    features = keep.shape[1]
    return pl.pallas_call(
        functools.partial(add_kernel, size, places),
        out_shape=jax.ShapeDtypeStruct((size, features), jnp.bfloat16),
        in_specs=[VMEM] * (1 + len(terms)),
        out_specs=VMEM,
        compiler_params=pltpu.CompilerParams(vmem_limit_bytes=16 * MIB),
        cost_estimate=pl.CostEstimate(flops=size * features, bytes_accessed=8 * size * features, transcendentals=0),
        name="add_rows",
    )(keep, *terms)


def mix_kernel(fars, share_ref, *refs):
    backs, out_ref = refs[:-1], refs[-1]
    steps, tokens, _ = out_ref.shape
    share = share_ref[...]
    total = sum(share[:, far:far + 1] * back[...].astype(jnp.float32) for far, back in zip(fars, backs))
    for step in range(steps):
        out_ref[step] = total[step * tokens:(step + 1) * tokens].astype(out_ref.dtype)


def mix(share, backs, shape):
    return pl.pallas_call(
        functools.partial(mix_kernel, tuple(backs)),
        out_shape=jax.ShapeDtypeStruct(shape, jnp.bfloat16),
        in_specs=[VMEM] * (1 + len(backs)),
        out_specs=VMEM,
        compiler_params=pltpu.CompilerParams(vmem_limit_bytes=16 * MIB),
        name="mix",
    )(share, *backs.values())


def local(hidden, expert_ids, route_weight, w_gate, w_up, w_down):
    step_count, token_count, features = hidden.shape
    slice_units = w_gate.shape[-1]
    splits = FF // slice_units
    devices = lax.axis_size("ep")
    experts = devices // splits
    row_count = step_count * token_count
    own_expert = lax.axis_index("ep") // splits

    last = devices - splits
    near, half = splits + 2, devices // 2
    direct = [key for key in range(devices - 1, 0, -1) if key & (key - 1) == 0 and key > 1] + [last + 2, near]
    blocks = {0: hidden}
    for key in direct:
        blocks[key] = swap(hidden, key, devices)
    blocks[half], blocks[splits] = lax.optimization_barrier((blocks[half], blocks[splits]))
    sources = dict(blocks)
    sources[half] = pass_rows(blocks[half], w_gate, w_up, w_down)
    for key in sorted(range(2, devices, 2), key=lambda key: (key.bit_count(), -key)):
        if key not in blocks:
            blocks[key] = sources[key] = swap(sources[key & (key - 1)], key & -key, devices)
    batches = [[*range(0, last, splits)], [2, near, last + 2]]
    batches.append([key for key in range(2, devices, 2) if key not in batches[0] + batches[1]])
    keep_rows = [pack([blocks[key] for key in keys]) for keys in batches]
    send_rows = [swap(rows, 1, devices) for rows in keep_rows]

    backs = {}
    fars = [0, *range(3, experts), 1, 2]
    keys = [key for batch in batches for key in batch]
    send, keep = expert_slice(keep_rows + send_rows, w_gate[0], w_up[0], w_down[0])
    twin = swap(send, 1, devices)
    for far in reversed(fars):
        theirs, mine = keys.index(far * splits + 2), keys.index(far * splits)
        across = swap(add_rows(row_count, (theirs, theirs), keep, twin), 2, devices)
        rows = add_rows(row_count, (mine, mine, 0), keep, twin, across)
        backs[far] = swap(rows, splits * far, devices) if far else rows

    weights = route_scale * route_weight / jnp.sum(route_weight, axis=-1, keepdims=True)
    away = own_expert ^ jnp.arange(experts, dtype=jnp.int32)
    share = jnp.sum(jnp.where(expert_ids[..., None] == away, weights[..., None], 0.0), axis=-2)
    return mix(share.reshape(row_count, experts), {far: backs[far] for far in fars}, hidden.shape)


def solution(mesh):
    placed = (
        P(None, ("groups", "ep"), None),
        P(None, ("groups", "ep"), None),
        P(None, ("groups", "ep"), None),
        P("ep", None, None),
        P("ep", None, None),
        P("ep", None, None),
    )
    return jax.shard_map(
        local,
        mesh=mesh,
        in_specs=placed,
        out_specs=P(None, ("groups", "ep"), None),
        check_vma=False,
    )
```

```python
import functools

import jax
import jax.numpy as jnp
from jax import lax
from jax.experimental import pallas as pl
from jax.experimental.pallas import tpu as pltpu
from jax.sharding import PartitionSpec as P

FF = 1024


route_scale = 2.5
MIB = 1 << 20
VMEM = pl.BlockSpec(memory_space=pltpu.VMEM)


def swap(value, mask, devices):
    return lax.ppermute(value, "ep", [(i, i ^ mask) for i in range(devices)])


def largest_chunk(total, most):
    return max(c for c in range(128, most + 1, 128) if total % c == 0)


def in_steps(total, depth, unrolled):
    def run(body):
        if unrolled:
            for step in range(total // depth):
                body(pl.ds(step * depth, depth))
        else:
            pl.loop(0, total // depth)(lambda step: body(pl.ds(pl.multiple_of(step * depth, depth), depth)))

    return run


def expert_kernel(count, size, first, *refs):
    blocks, (gate_ref, up_ref, down_ref, first_ref, rest_ref, keep_ref, both) = refs[:count], refs[count:]
    features, units = gate_ref.shape[-2:]
    depth = largest_chunk(features, 1024)
    half = keep_ref.shape[0]
    pieces = range(half // size)
    chosen = [(first_ref, first), (rest_ref, [piece for piece in pieces if piece not in first])]
    both[...] = jnp.zeros_like(both)

    @in_steps(features, depth, both.shape[1] <= 256)
    def _(at):
        rows = jnp.concatenate([block[:, at] for block in blocks], axis=0)
        both[0] += jnp.dot(rows, gate_ref[at, :], preferred_element_type=jnp.float32)
        both[1] += jnp.dot(rows, up_ref[at, :], preferred_element_type=jnp.float32)

    gate_pre = both[0]
    slice_hidden = (gate_pre / (1 + jnp.exp(-gate_pre)) * both[1]).astype(jnp.bfloat16)

    @in_steps(features, depth, both.shape[1] <= 256)
    def _(at):
        out = jnp.dot(slice_hidden, down_ref[:, at], preferred_element_type=jnp.float32)
        keep_ref[:, at] = out[:half]
        for ref, places in chosen:
            rows = [out[half + place * size:half + (place + 1) * size] for place in places]
            ref[:, at] = jnp.concatenate(rows, axis=0).astype(jnp.bfloat16)


def expert_slice(blocks, size, first, gate_w, up_w, down_w):
    features, units = gate_w.shape
    rows = sum(block.shape[0] for block in blocks)
    half = rows // 2
    return pl.pallas_call(
        functools.partial(expert_kernel, len(blocks), size, first),
        out_shape=(
            jax.ShapeDtypeStruct((len(first) * size, features), jnp.bfloat16),
            jax.ShapeDtypeStruct((half - len(first) * size, features), jnp.bfloat16),
            jax.ShapeDtypeStruct((half, features), jnp.float32),
        ),
        in_specs=[VMEM] * (len(blocks) + 3),
        out_specs=(VMEM, VMEM, VMEM),
        scratch_shapes=[pltpu.VMEM((2, rows, units), jnp.float32)],
        compiler_params=pltpu.CompilerParams(vmem_limit_bytes=28 * MIB),
        cost_estimate=pl.CostEstimate(flops=6 * rows * units * features, bytes_accessed=6 * units * features, transcendentals=0),
        name="expert_slice",
    )(*blocks, gate_w, up_w, down_w)


def pass_kernel(rows_ref, *refs):
    refs[-1][...] = rows_ref[...]


def pass_rows(rows, *beside):
    return pl.pallas_call(
        pass_kernel,
        out_shape=jax.ShapeDtypeStruct(rows.shape, rows.dtype),
        in_specs=[VMEM] + [pl.BlockSpec(memory_space=pl.ANY)] * len(beside),
        out_specs=VMEM,
        compiler_params=pltpu.CompilerParams(vmem_limit_bytes=16 * MIB),
        name="pass_rows",
    )(rows, *[pltpu.with_memory_space_constraint(w, pltpu.HBM) for w in beside])


def pack_kernel(*refs):
    refs[-1][...] = jnp.concatenate([ref[step] for ref in refs[:-1] for step in range(ref.shape[0])], axis=0)


def pack(blocks):
    steps, tokens, features = blocks[0].shape
    rows = len(blocks) * steps * tokens
    return pl.pallas_call(
        pack_kernel,
        out_shape=jax.ShapeDtypeStruct((rows, features), blocks[0].dtype),
        in_specs=[VMEM] * len(blocks),
        out_specs=VMEM,
        compiler_params=pltpu.CompilerParams(vmem_limit_bytes=16 * MIB),
        cost_estimate=pl.CostEstimate(flops=0, bytes_accessed=4 * rows * features, transcendentals=0),
        name="pack_rows",
    )(*blocks)


def add_kernel(size, places, keep_ref, *refs):
    terms, out_ref = refs[:-1], refs[-1]
    total = keep_ref[pl.ds(places[0] * size, size), :]
    for place, term in zip(places[1:], terms):
        total = total + term[pl.ds(place * size, size), :].astype(jnp.float32)
    out_ref[...] = total.astype(out_ref.dtype)


def add_rows(size, places, keep, *terms):
    features = keep.shape[1]
    return pl.pallas_call(
        functools.partial(add_kernel, size, places),
        out_shape=jax.ShapeDtypeStruct((size, features), jnp.bfloat16),
        in_specs=[VMEM] * (1 + len(terms)),
        out_specs=VMEM,
        compiler_params=pltpu.CompilerParams(vmem_limit_bytes=16 * MIB),
        cost_estimate=pl.CostEstimate(flops=size * features, bytes_accessed=8 * size * features, transcendentals=0),
        name="add_rows",
    )(keep, *terms)


def mix_kernel(fars, share_ref, *refs):
    backs, out_ref = refs[:-1], refs[-1]
    steps, tokens, _ = out_ref.shape
    share = share_ref[...]
    total = sum(share[:, far:far + 1] * back[...].astype(jnp.float32) for far, back in zip(fars, backs))
    for step in range(steps):
        out_ref[step] = total[step * tokens:(step + 1) * tokens].astype(out_ref.dtype)


def mix(share, backs, shape):
    return pl.pallas_call(
        functools.partial(mix_kernel, tuple(backs)),
        out_shape=jax.ShapeDtypeStruct(shape, jnp.bfloat16),
        in_specs=[VMEM] * (1 + len(backs)),
        out_specs=VMEM,
        compiler_params=pltpu.CompilerParams(vmem_limit_bytes=16 * MIB),
        name="mix",
    )(share, *backs.values())


def local(hidden, expert_ids, route_weight, w_gate, w_up, w_down):
    step_count, token_count, features = hidden.shape
    slice_units = w_gate.shape[-1]
    splits = FF // slice_units
    devices = lax.axis_size("ep")
    experts = devices // splits
    row_count = step_count * token_count
    own_expert = lax.axis_index("ep") // splits

    last = devices - splits
    near, half = splits + 2, devices // 2
    direct = [key for key in range(devices - 1, 0, -1) if key & (key - 1) == 0 and key > 1] + [last + 2, near]
    blocks = {0: hidden}
    for key in direct:
        blocks[key] = swap(hidden, key, devices)
    blocks[half], blocks[splits] = lax.optimization_barrier((blocks[half], blocks[splits]))
    sources = dict(blocks)
    sources[half] = pass_rows(blocks[half], w_gate, w_up, w_down)
    for key in sorted(range(2, devices, 2), key=lambda key: (key.bit_count(), -key)):
        if key not in blocks:
            blocks[key] = sources[key] = swap(sources[key & (key - 1)], key & -key, devices)
    batches = [[*range(0, last, splits)], [2, near, last + 2]]
    batches.append([key for key in range(2, devices, 2) if key not in batches[0] + batches[1]])
    keep_rows = [pack([blocks[key] for key in keys]) for keys in batches]
    send_rows = [swap(rows, 1, devices) for rows in keep_rows]

    fars = [0, *range(3, experts), 1, 2]
    keys = [key for batch in batches for key in batch]
    first = [keys.index(fars[-1] * splits), keys.index(fars[-1] * splits + 2)]
    rest = [place for place in range(len(keys)) if place not in first]
    *sends, keep = expert_slice(keep_rows + send_rows, row_count, first, w_gate[0], w_up[0], w_down[0])
    twins = [swap(sends[0], 1, devices)]
    twins[0], sends[1] = lax.optimization_barrier((twins[0], sends[1]))
    twins.append(swap(sends[1], 1, devices))
    backs = {}
    for far in reversed(fars):
        mine, theirs = keys.index(far * splits), keys.index(far * splits + 2)
        twin, there = (twins[0], first) if mine in first else (twins[1], rest)
        across = swap(add_rows(row_count, (theirs, there.index(theirs)), keep, twin), 2, devices)
        rows = add_rows(row_count, (mine, there.index(mine), 0), keep, twin, across)
        backs[far] = swap(rows, splits * far, devices) if far else rows

    weights = route_scale * route_weight / jnp.sum(route_weight, axis=-1, keepdims=True)
    away = own_expert ^ jnp.arange(experts, dtype=jnp.int32)
    share = jnp.sum(jnp.where(expert_ids[..., None] == away, weights[..., None], 0.0), axis=-2)
    return mix(share.reshape(row_count, experts), {far: backs[far] for far in fars}, hidden.shape)


def solution(mesh):
    placed = (
        P(None, ("groups", "ep"), None),
        P(None, ("groups", "ep"), None),
        P(None, ("groups", "ep"), None),
        P("ep", None, None),
        P("ep", None, None),
        P("ep", None, None),
    )
    return jax.shard_map(
        local,
        mesh=mesh,
        in_specs=placed,
        out_specs=P(None, ("groups", "ep"), None),
        check_vma=False,
    )
```
